32 devices in a mesh: sup: 2 (over y), row: 8 (over z, x), col: 2 (over core).
Axes of the slice: x: 2, y: 2, z: 4, core: 2. Of those that a mesh axis runs over, the one named last changes fastest.
Arguments:
- schur_block: float32 [24576, 12288], P(('sup', 'row'), 'col'), parts along dimension 0, may hold values from -6 to 6
- w_first: bfloat16 [80, 12288], P(('sup', 'row'), 'col'), parts along dimension 0, may hold values from -2 to 2
- w_second: bfloat16 [80, 12288], P(('sup', 'row'), 'col'), parts along dimension 0, may hold values from -2 to 2
Outputs:
- condensed: float32 [24576, 12288], P(('sup', 'row'), 'col'), parts along dimension 0
The draws below stay inside these ranges and needn't reach their ends.
There are 2 independent parts, one for each index of `sup`. The reference program is written for one: setup_inputs(seed, part) draws one part's arguments, and reference() takes and returns one part's arrays. A program takes and returns all parts, laid end to end along the dimension named above; each array names one. Nothing has to cross between parts.
All inputs are finite; a program needn't handle non-finite values.
Results may differ from the reference program's by a relative error of at most 0.0003.
Values may be sent and summed in bfloat16 or wider, within the bound.
No kernel may reach another device: no remote copies, remote signals or barrier semaphores. Data moves between devices by JAX's collectives and lax.ppermute only.
A program may use at most 192 MiB of HBM per device.

```python
import jax
import jax.numpy as jnp
from jax import lax

NB = 12288
KS = 40


def steps_of(own_key, extent, pieces, smallest, top_value):
    loudness, own = 1.0, jax.random.fold_in(own_key, 6)
    for position, parts in pieces:
        steps = jnp.exp(jax.random.uniform(jax.random.fold_in(own, position), (parts,), jnp.float32, smallest / len(pieces), top_value / len(pieces)))
        loudness = loudness * jnp.repeat(steps, extent[position] // parts).reshape([-1 if axis == position else 1 for axis in range(len(extent))])
    return loudness


def bell_draw(key, extent, scale, limit, pieces=(), kind=jnp.bfloat16):
    entries = jax.random.normal(key, extent, jnp.float32) * scale
    if len(pieces) > 0:
        entries = steps_of(key, extent, pieces, -0.22, 0.18) * entries
    return jnp.clip(entries, min=-limit, max=limit).astype(kind)


def setup_inputs(seed: int = 0, part: int = 0) -> dict:
    streams_of = jax.random.split(jax.random.key(seed), 4)
    part_keys = jax.random.split(jax.random.fold_in(streams_of[3], part), 4)
    return {
        "schur_block": bell_draw(part_keys[0], (NB, NB), 1.0, 6.0, ((0, 8), (1, 2)), jnp.float32),
        "w_first": bell_draw(part_keys[1], (KS, NB), 0.15, 2.0, ((0, 8), (1, 2))),
        "w_second": bell_draw(part_keys[2], (KS, NB), 0.15, 2.0, ((0, 8), (1, 2))),
    }


def gram(slab):
    return lax.dot_general(slab, slab, (((0,), (0,)), ((), ())), preferred_element_type=jnp.float32)


def reference(schur_block, w_first, w_second):
    update = gram(w_first) + gram(w_second)
    return schur_block - update
```

```python
import functools

import jax
import jax.numpy as jnp
from jax import lax
from jax.experimental import pallas as pl
from jax.experimental.pallas import tpu as pltpu
from jax.sharding import PartitionSpec as P

MIB = 1 << 20
WHOLE = pl.BlockSpec(memory_space=pltpu.VMEM)


def in_vmem(array):
    return pltpu.with_memory_space_constraint(array, pltpu.VMEM)


class Packing:
    def __init__(self, rows, width):
        self.rows, self.width = rows, width
        self.full = rows // 8 * 8
        self.rest = rows - self.full
        self.fold = 8 // self.rest if self.rest else 1
        assert self.rest == 0 or (8 % self.rest == 0 and self.full == 8)
        assert width % (128 * self.fold) == 0
        self.chunk = width // self.fold
        self.packed = (self.full, width + (self.chunk if self.rest else 0))


def pack_kernel(packing, first_ref, second_ref, out_ref):
    local = first_ref.shape[0]
    both = jnp.concatenate([first_ref[...], second_ref[...]], axis=0)
    out_ref[:, : packing.width] = both[: packing.full]
    for i in range(packing.fold if packing.rest else 0):
        lanes = slice(i * packing.chunk, (i + 1) * packing.chunk)
        out_ref[i * packing.rest : (i + 1) * packing.rest, packing.width :] = both[packing.full :, lanes]


def pack(packing, first, second):
    return pl.pallas_call(
        functools.partial(pack_kernel, packing),
        in_specs=[WHOLE] * 2,
        out_specs=WHOLE,
        out_shape=jax.ShapeDtypeStruct(packing.packed, first.dtype),
        compiler_params=pltpu.CompilerParams(vmem_limit_bytes=8 * MIB),
        name="pack",
    )(first, second)


def gather_rows(block, axis):
    count = lax.axis_size(axis)
    if count > 16 or count % 2:
        return [lax.all_gather(block, axis, axis=0)]
    ring = [2 * i for i in range(count // 2)] + [2 * i + 1 for i in reversed(range(count // 2))]
    place = {index: position for position, index in enumerate(ring)}

    def step(array, by):
        return lax.ppermute(array, axis, [(i, ring[(place[i] + by) % count]) for i in range(count)])

    blocks, ahead, behind = [block], block, block
    for hop in range(1, count // 2 + 1):
        ahead = step(ahead, 1)
        blocks.append(ahead)
        if hop < (count + 1) // 2:
            behind = step(behind, -1)
            blocks.append(behind)
    return [b[None] for b in blocks]


def assemble_kernel(packing, tile, per_column, *refs):
    *piece_refs, right_ref, left_ref = refs
    count = sum(ref.shape[0] for ref in piece_refs)
    at = 0
    for ref in piece_refs:
        for p in range(ref.shape[0]):
            right_ref[at * packing.full : (at + 1) * packing.full, :] = ref[p, :, : packing.width]
            for i in range(packing.fold if packing.rest else 0):
                lanes = slice(i * packing.chunk, (i + 1) * packing.chunk)
                low = count * packing.full + at * packing.rest
                right_ref[low : low + packing.rest, lanes] = ref[
                    p, i * packing.rest : (i + 1) * packing.rest, packing.width :
                ]
            at += 1
    start = pl.multiple_of(lax.axis_index("row") % per_column * tile, 128)
    left_ref[...] = right_ref[:, pl.ds(start, tile)]


def assemble(packing, pieces, tile, per_column):
    depth = packing.rows * sum(p.shape[0] for p in pieces)
    dtype = pieces[0].dtype
    return pl.pallas_call(
        functools.partial(assemble_kernel, packing, tile, per_column),
        in_specs=[WHOLE] * len(pieces),
        out_specs=(WHOLE, WHOLE),
        out_shape=(pltpu.VMEM((depth, packing.width), dtype), pltpu.VMEM((depth, tile), dtype)),
        compiler_params=pltpu.CompilerParams(vmem_limit_bytes=16 * MIB),
        name="assemble",
    )(*[in_vmem(p) for p in pieces])


def assemble_plain(packing, pieces, tile, per_column):
    stack = jnp.concatenate(pieces, axis=0)
    count = stack.shape[0]
    top = stack[:, :, : packing.width].reshape(count * packing.full, packing.width)
    rest = stack[:, :, packing.width :].reshape(count, packing.fold, packing.rest, packing.chunk)
    rest = jnp.transpose(rest, (0, 2, 1, 3)).reshape(count * packing.rest, packing.width)
    right = jnp.concatenate([top, rest], axis=0)
    start = lax.axis_index("row") % per_column * tile
    return right, lax.dynamic_slice(right, (0, start), (right.shape[0], tile))


def update_kernel(block, slots, per_column, schur_ref, own_ref, peer_ref, right_ref, out_ref, left, right, stage, sems):
    rows, columns = block
    depth, width = right_ref.shape
    padded = right.shape[0]
    down, across = out_ref.shape[0] // rows, width // columns
    steps = down * across
    owner = lax.axis_index("col") == lax.axis_index("row") // per_column

    if padded > depth:
        left[:, depth:] = jnp.zeros((left.shape[0], padded - depth), left.dtype)
        right[depth:, :] = jnp.zeros((padded - depth, width), right.dtype)
    right[:depth, :] = right_ref[...]

    @pl.when(owner)
    def _():
        left[:, :depth] = own_ref[...].T

    @pl.when(jnp.logical_not(owner))
    def _():
        left[:, :depth] = peer_ref[...].T

    def place(t):
        i, j = t // across, t % across
        return pl.ds(pl.multiple_of(i * rows, rows), rows), pl.ds(pl.multiple_of(j * columns, columns), columns)

    def copy(t, slot):
        return pltpu.make_async_copy(stage.at[slot], out_ref.at[place(t)], sems.at[slot])

    def step(t, _):
        slot = t % slots

        @pl.when(t >= slots)
        def _():
            copy(t - slots, slot).wait()

        at_rows, at_columns = place(t)
        update = jnp.dot(left[at_rows, :], right[:, at_columns], preferred_element_type=jnp.float32)
        stage[slot] = schur_ref[at_rows, at_columns] - update
        copy(t, slot).start()
        return 0

    lax.fori_loop(0, steps, step, 0)
    for t in range(max(0, steps - slots), steps):
        copy(t, t % slots).wait()


def update(schur, own, peer, right, per_column):
    tile, width = schur.shape
    depth = right.shape[0]
    padded = -(-depth // 128) * 128
    rows = next(r for r in (512, 384, 256, 128, tile) if tile % r == 0)
    columns = next(c for c in (512, 384, 256, 128, width) if width % c == 0)
    slots = 6
    scratch = 4 * slots * rows * columns + 2 * padded * (tile + width)
    return pl.pallas_call(
        functools.partial(update_kernel, (rows, columns), slots, per_column),
        in_specs=[WHOLE] * 4,
        out_specs=pl.BlockSpec(memory_space=pl.ANY),
        out_shape=jax.ShapeDtypeStruct(schur.shape, schur.dtype),
        scratch_shapes=[
            pltpu.VMEM((tile, padded), right.dtype),
            pltpu.VMEM((padded, width), right.dtype),
            pltpu.VMEM((slots, rows, columns), jnp.float32),
            pltpu.SemaphoreType.DMA((slots,)),
        ],
        compiler_params=pltpu.CompilerParams(vmem_limit_bytes=scratch + 6 * MIB),
        name="update",
    )(in_vmem(schur), in_vmem(own), in_vmem(peer), in_vmem(right))


def per_device(schur_block, w_first, w_second):
    row_count = lax.axis_size("row")
    col_count = lax.axis_size("col")
    tile, width = schur_block.shape
    per_column = row_count // col_count
    packing = Packing(w_first.shape[0] + w_second.shape[0], width)
    pieces = gather_rows(pack(packing, w_first, w_second), "row")
    build = assemble if tile % 128 == 0 else assemble_plain
    right, own = build(packing, pieces, tile, per_column)
    peer = lax.ppermute(own, "col", [(c, (c + 1) % col_count) for c in range(col_count)])
    return update(schur_block, own, peer, right, per_column)


def solution(mesh):
    assert mesh.shape["col"] == 2
    placed = P(("sup", "row"), "col")
    return jax.shard_map(per_device, mesh=mesh, in_specs=(placed,) * 3, out_specs=placed, check_vma=False)
```

```python
import functools

import jax
import jax.numpy as jnp
from jax import lax
from jax.experimental import pallas as pl
from jax.experimental.pallas import tpu as pltpu
from jax.sharding import PartitionSpec as P

MIB = 1 << 20
WHOLE = pl.BlockSpec(memory_space=pltpu.VMEM)
ANYWHERE = pl.BlockSpec(memory_space=pl.ANY)
IN_HBM = pl.BlockSpec(memory_space=pltpu.HBM)
SHARES = ([5, 5, 5, 5], 2, 2)
COLS = 1024


def in_vmem(array):
    return pltpu.with_memory_space_constraint(array, pltpu.VMEM)


def in_hbm(array):
    return pltpu.with_memory_space_constraint(array, pltpu.HBM)


class Packing:
    def __init__(self, rows, width):
        self.rows, self.width = rows, width
        self.full = rows // 8 * 8
        self.rest = rows - self.full
        self.fold = 8 // self.rest if self.rest else 1
        assert self.rest == 0 or (8 % self.rest == 0 and self.full == 8)
        assert width % (128 * self.fold) == 0
        self.chunk = width // self.fold
        self.packed = (self.full, width + (self.chunk if self.rest else 0))


def pack_kernel(packing, first_hbm, second_hbm, out_ref, first_ref, second_ref, sems):
    copies = [
        pltpu.make_async_copy(first_hbm, first_ref, sems.at[0]),
        pltpu.make_async_copy(second_hbm, second_ref, sems.at[1]),
    ]
    for copy in copies:
        copy.start()
    for copy in copies:
        copy.wait()
    both = jnp.concatenate([first_ref[...], second_ref[...]], axis=0)
    out_ref[:, : packing.width] = both[: packing.full]
    for i in range(packing.fold if packing.rest else 0):
        lanes = slice(i * packing.chunk, (i + 1) * packing.chunk)
        out_ref[i * packing.rest : (i + 1) * packing.rest, packing.width :] = both[packing.full :, lanes]


def pack(packing, first, second):
    return pl.pallas_call(
        functools.partial(pack_kernel, packing),
        in_specs=[IN_HBM] * 2,
        out_specs=WHOLE,
        out_shape=pltpu.VMEM(packing.packed, first.dtype),
        scratch_shapes=[
            pltpu.VMEM(first.shape, first.dtype),
            pltpu.VMEM(second.shape, second.dtype),
            pltpu.SemaphoreType.DMA((2,)),
        ],
        compiler_params=pltpu.CompilerParams(vmem_limit_bytes=8 * MIB),
        name="pack",
    )(in_hbm(first), in_hbm(second))


def fetch_kernel(low, schur_ref, token_ref, out_ref, sem):
    copy = pltpu.make_async_copy(schur_ref.at[pl.ds(low, out_ref.shape[0]), :], out_ref, sem)
    copy.start()
    copy.wait()


def fetch(schur, low, rows, token):
    width = schur.shape[1]
    return pl.pallas_call(
        functools.partial(fetch_kernel, low),
        in_specs=[IN_HBM, ANYWHERE],
        out_specs=WHOLE,
        out_shape=pltpu.VMEM((rows, width), schur.dtype),
        scratch_shapes=[pltpu.SemaphoreType.DMA],
        cost_estimate=pl.CostEstimate(flops=0, transcendentals=0, bytes_accessed=8 * rows * width),
        compiler_params=pltpu.CompilerParams(vmem_limit_bytes=MIB),
        name="fetch",
    )(in_hbm(schur), token)


def shares_of(rows, hops):
    by_hop, by_swap, late = SHARES
    unit = rows // (sum(by_hop) + by_swap + late)
    if hops != len(by_hop) or unit % 16 or unit * (sum(by_hop) + by_swap + late) != rows:
        return [], rows
    return [s * unit for s in by_hop], by_swap * unit


def gather_rows(block, axis, schur, sizes):
    count = lax.axis_size(axis)
    if not sizes:
        return [lax.all_gather(block, axis, axis=0)], []
    ring = [2 * i for i in range(count // 2)] + [2 * i + 1 for i in reversed(range(count // 2))]
    place = {index: position for position, index in enumerate(ring)}

    def step(array, by):
        return lax.ppermute(array, axis, [(i, ring[(place[i] + by) % count]) for i in range(count)])

    blocks, ahead, behind, fetched = [block], block, block, []
    for hop in range(count // 2):
        part = fetch(schur, sum(sizes[:hop]), sizes[hop], ahead)
        ahead = step(ahead, 1)
        if hop < count // 2 - 1:
            behind = step(behind, -1)
        ahead, part = lax.optimization_barrier((ahead, part))
        if hop < count // 2 - 1:
            behind, part = lax.optimization_barrier((behind, part))
        blocks.append(ahead)
        if hop < count // 2 - 1:
            blocks.append(behind)
        fetched.append(part)
    return [b[None] for b in blocks], fetched


def assemble_kernel(packing, tile, per_column, *refs):
    *piece_refs, right_ref, left_ref = refs
    count = sum(ref.shape[0] for ref in piece_refs)
    at = 0
    for ref in piece_refs:
        for p in range(ref.shape[0]):
            right_ref[at * packing.full : (at + 1) * packing.full, :] = ref[p, :, : packing.width]
            for i in range(packing.fold if packing.rest else 0):
                lanes = slice(i * packing.chunk, (i + 1) * packing.chunk)
                low = count * packing.full + at * packing.rest
                right_ref[low : low + packing.rest, lanes] = ref[
                    p, i * packing.rest : (i + 1) * packing.rest, packing.width :
                ]
            at += 1
    start = pl.multiple_of(lax.axis_index("row") % per_column * tile, 128)
    left_ref[...] = right_ref[:, pl.ds(start, tile)]


def assemble(packing, pieces, tile, per_column):
    depth = packing.rows * sum(p.shape[0] for p in pieces)
    dtype = pieces[0].dtype
    return pl.pallas_call(
        functools.partial(assemble_kernel, packing, tile, per_column),
        in_specs=[WHOLE] * len(pieces),
        out_specs=(WHOLE, WHOLE),
        out_shape=(pltpu.VMEM((depth, packing.width), dtype), pltpu.VMEM((depth, tile), dtype)),
        compiler_params=pltpu.CompilerParams(vmem_limit_bytes=8 * MIB),
        name="assemble",
    )(*[in_vmem(p) for p in pieces])


def assemble_plain(packing, pieces, tile, per_column):
    stack = jnp.concatenate(pieces, axis=0)
    count = stack.shape[0]
    top = stack[:, :, : packing.width].reshape(count * packing.full, packing.width)
    rest = stack[:, :, packing.width :].reshape(count, packing.fold, packing.rest, packing.chunk)
    rest = jnp.transpose(rest, (0, 2, 1, 3)).reshape(count * packing.rest, packing.width)
    right = jnp.concatenate([top, rest], axis=0)
    start = lax.axis_index("row") % per_column * tile
    return right, lax.dynamic_slice(right, (0, start), (right.shape[0], tile))


def update_kernel(columns, per_column, schur_hbm, own_ref, peer_ref, right_ref, *refs):
    count = (len(refs) - 5) // 2
    parts, out_ref, held = refs[:count], refs[count], list(refs[count + 1 : 2 * count + 1])
    left, late, sems, late_sem = refs[2 * count + 1 :]
    width = out_ref.shape[1]
    late_rows = out_ref.shape[0] - sum(part.shape[0] for part in parts)
    owner = lax.axis_index("col") == lax.axis_index("row") // per_column
    if late_rows:
        fill = pltpu.make_async_copy(schur_hbm.at[pl.ds(out_ref.shape[0] - late_rows, late_rows), :], late, late_sem)
        fill.start()
        parts, held = [*parts, late], [*held, late]
    steps = width // columns
    lows = [sum(part.shape[0] for part in parts[:i]) for i in range(len(parts))]

    def copy(number, t):
        rows = parts[number].shape[0]
        lanes = pl.ds(pl.multiple_of(t * columns, columns), columns)
        return pltpu.make_async_copy(
            held[number].at[:, lanes], out_ref.at[pl.ds(lows[number], rows), lanes], sems.at[number, t]
        )

    for number, part in enumerate(parts):
        low, rows = lows[number], part.shape[0]

        @pl.when(owner)
        def _():
            left[:rows, :] = own_ref[:, low : low + rows].T

        @pl.when(jnp.logical_not(owner))
        def _():
            left[:rows, :] = peer_ref[:, low : low + rows].T

        if late_rows and number == len(parts) - 1:
            fill.wait()

        def step(t, _):
            lanes = pl.ds(pl.multiple_of(t * columns, columns), columns)
            update = jnp.dot(left[:rows, :], right_ref[:, lanes], preferred_element_type=jnp.float32)
            held[number][:, lanes] = part[:, lanes] - update
            copy(number, t).start()
            return 0

        lax.fori_loop(0, steps, step, 0)
    for number in range(len(parts)):
        for t in range(steps):
            copy(number, t).wait()


def update(schur, parts, own, peer, right, per_column):
    depth, width = right.shape
    tile = schur.shape[0]
    late_rows = tile - sum(part.shape[0] for part in parts)
    columns = next(c for c in (COLS, 256, 128) if width % c == 0)
    most = max([part.shape[0] for part in parts] + [late_rows])
    scratch = 2 * most * max(depth, 128) + 4 * late_rows * width
    result, *_ = pl.pallas_call(
        functools.partial(update_kernel, columns, per_column),
        in_specs=[IN_HBM] + [WHOLE] * (3 + len(parts)),
        out_specs=[ANYWHERE] + [WHOLE] * len(parts),
        out_shape=[jax.ShapeDtypeStruct(schur.shape, schur.dtype)] + [pltpu.VMEM(p.shape, p.dtype) for p in parts],
        input_output_aliases={4 + i: 1 + i for i in range(len(parts))},
        scratch_shapes=[
            pltpu.VMEM((most, depth), right.dtype),
            pltpu.VMEM((late_rows or 8, width), jnp.float32),
            pltpu.SemaphoreType.DMA((len(parts) + 1, width // columns)),
            pltpu.SemaphoreType.DMA,
        ],
        compiler_params=pltpu.CompilerParams(vmem_limit_bytes=scratch + 4 * MIB),
        name="update",
    )(in_hbm(schur), *[in_vmem(a) for a in (own, peer, right, *parts)])
    return result


def per_device(schur_block, w_first, w_second):
    row_count = lax.axis_size("row")
    col_count = lax.axis_size("col")
    tile, width = schur_block.shape
    per_column = row_count // col_count
    packing = Packing(w_first.shape[0] + w_second.shape[0], width)
    sizes, beside_swap = shares_of(tile, row_count // 2)
    pieces, parts = gather_rows(pack(packing, w_first, w_second), "row", schur_block, sizes)
    build = assemble if tile % 128 == 0 else assemble_plain
    right, own = build(packing, pieces, tile, per_column)
    if beside_swap:
        parts = [*parts, fetch(schur_block, sum(sizes), beside_swap, own)]
    peer = lax.ppermute(own, "col", [(c, (c + 1) % col_count) for c in range(col_count)])
    return update(schur_block, parts, own, peer, right, per_column)


def solution(mesh):
    assert mesh.shape["col"] == 2
    placed = P(("sup", "row"), "col")
    return jax.shard_map(per_device, mesh=mesh, in_specs=(placed,) * 3, out_specs=placed, check_vma=False)
```

```python
import functools

import jax
import jax.numpy as jnp
from jax import lax
from jax.experimental import pallas as pl
from jax.experimental.pallas import tpu as pltpu
from jax.sharding import PartitionSpec as P

MIB = 1 << 20
WHOLE = pl.BlockSpec(memory_space=pltpu.VMEM)
ANYWHERE = pl.BlockSpec(memory_space=pl.ANY)
IN_HBM = pl.BlockSpec(memory_space=pltpu.HBM)
SHARES = ([11, 11, 18], 4, 4)
COLS = 1024
EARLY = 192


def in_vmem(array):
    return pltpu.with_memory_space_constraint(array, pltpu.VMEM)


def in_hbm(array):
    return pltpu.with_memory_space_constraint(array, pltpu.HBM)


class Packing:
    def __init__(self, rows, width):
        self.rows, self.width = rows, width
        self.full = rows // 8 * 8
        self.rest = rows - self.full
        self.fold = 8 // self.rest if self.rest else 1
        assert self.rest == 0 or (8 % self.rest == 0 and self.full == 8)
        assert width % (128 * self.fold) == 0
        self.chunk = width // self.fold
        self.packed = (self.full, width + (self.chunk if self.rest else 0))


def is_early():
    return jnp.logical_and(lax.axis_index("sup") == 0, lax.axis_index("row") == 0)


def pack_kernel(packing, low, first_hbm, second_hbm, schur_hbm, out_ref, room_ref, first_ref, second_ref, sems):
    copies = [
        pltpu.make_async_copy(first_hbm, first_ref, sems.at[0]),
        pltpu.make_async_copy(second_hbm, second_ref, sems.at[1]),
    ]
    for copy in copies:
        copy.start()
    rows = min(EARLY, room_ref.shape[0])
    ahead = pltpu.make_async_copy(schur_hbm.at[pl.ds(low, rows), :], room_ref.at[pl.ds(0, rows), :], sems.at[2])
    pl.when(is_early())(ahead.start)
    for copy in copies:
        copy.wait()
    both = jnp.concatenate([first_ref[...], second_ref[...]], axis=0)
    out_ref[:, : packing.width] = both[: packing.full]
    for i in range(packing.fold if packing.rest else 0):
        lanes = slice(i * packing.chunk, (i + 1) * packing.chunk)
        out_ref[i * packing.rest : (i + 1) * packing.rest, packing.width :] = both[packing.full :, lanes]
    pl.when(is_early())(ahead.wait)


def pack(packing, first, second, schur, low, rows):
    return pl.pallas_call(
        functools.partial(pack_kernel, packing, low),
        in_specs=[IN_HBM] * 3,
        out_specs=(WHOLE, WHOLE),
        out_shape=(pltpu.VMEM(packing.packed, first.dtype), pltpu.VMEM((rows, schur.shape[1]), schur.dtype)),
        scratch_shapes=[
            pltpu.VMEM(first.shape, first.dtype),
            pltpu.VMEM(second.shape, second.dtype),
            pltpu.SemaphoreType.DMA((3,)),
        ],
        compiler_params=pltpu.CompilerParams(vmem_limit_bytes=8 * MIB),
        name="pack",
    )(in_hbm(first), in_hbm(second), in_hbm(schur))


def fetch_kernel(low, schur_ref, token_ref, out_ref, sem):
    copy = pltpu.make_async_copy(schur_ref.at[pl.ds(low, out_ref.shape[0]), :], out_ref, sem)
    copy.start()
    copy.wait()


def fetch(schur, low, rows, token):
    width = schur.shape[1]
    return pl.pallas_call(
        functools.partial(fetch_kernel, low),
        in_specs=[IN_HBM, ANYWHERE],
        out_specs=WHOLE,
        out_shape=pltpu.VMEM((rows, width), schur.dtype),
        scratch_shapes=[pltpu.SemaphoreType.DMA],
        cost_estimate=pl.CostEstimate(flops=0, transcendentals=0, bytes_accessed=8 * rows * width),
        compiler_params=pltpu.CompilerParams(vmem_limit_bytes=MIB),
        name="fetch",
    )(in_hbm(schur), token)


def fill_kernel(low, schur_ref, token_ref, room_ref, out_ref, sem):
    rows = out_ref.shape[0]
    skip = min(EARLY, rows)

    def run(done):
        copy = pltpu.make_async_copy(
            schur_ref.at[pl.ds(low + done, rows - done), :], out_ref.at[pl.ds(done, rows - done), :], sem
        )
        copy.start()
        copy.wait()

    if rows > skip:
        pl.when(is_early())(functools.partial(run, skip))
    pl.when(jnp.logical_not(is_early()))(functools.partial(run, 0))


def fill(schur, low, room, token):
    rows, width = room.shape
    return pl.pallas_call(
        functools.partial(fill_kernel, low),
        in_specs=[IN_HBM, ANYWHERE, WHOLE],
        out_specs=WHOLE,
        out_shape=pltpu.VMEM(room.shape, room.dtype),
        input_output_aliases={2: 0},
        scratch_shapes=[pltpu.SemaphoreType.DMA],
        cost_estimate=pl.CostEstimate(flops=0, transcendentals=0, bytes_accessed=8 * rows * width),
        compiler_params=pltpu.CompilerParams(vmem_limit_bytes=MIB),
        name="fill",
    )(in_hbm(schur), token, in_vmem(room))


def shares_of(rows, hops):
    by_hop, by_swap, late = SHARES
    unit = rows // (sum(by_hop) + by_swap + late)
    if hops != 4 or unit % 16 or unit * (sum(by_hop) + by_swap + late) != rows:
        return [], rows
    return [s * unit for s in by_hop], by_swap * unit


def pick_kernel(count, ahead_ref, behind_ref, out_ref):
    index = lax.axis_index("row")
    end = (index >= count // 2) == (index % 2 == 1)

    @pl.when(end)
    def _():
        out_ref[...] = behind_ref[...]

    @pl.when(jnp.logical_not(end))
    def _():
        out_ref[...] = ahead_ref[...]


def pick(count, ahead, behind):
    return pl.pallas_call(
        functools.partial(pick_kernel, count),
        in_specs=[WHOLE] * 2,
        out_specs=WHOLE,
        out_shape=pltpu.VMEM(ahead.shape, ahead.dtype),
        compiler_params=pltpu.CompilerParams(vmem_limit_bytes=MIB),
        name="pick",
    )(in_vmem(ahead), in_vmem(behind))


def gather_rows(block, axis, schur, room, sizes):
    count = lax.axis_size(axis)
    if not sizes:
        return [lax.all_gather(block, axis, axis=0)], []
    assert count == 8
    ring = [2 * i for i in range(count // 2)] + [2 * i + 1 for i in reversed(range(count // 2))]
    place = {index: position for position, index in enumerate(ring)}

    def step(array, by):
        return lax.ppermute(array, axis, [(i, ring[(place[i] + by) % count]) for i in range(count)])

    blocks, ahead, behind, fetched = [block], block, block, []
    for hop in range(3):
        low = sum(sizes[:hop])
        part = fetch(schur, low, sizes[hop], ahead) if hop < 2 else fill(schur, low, room, ahead)
        if hop == 2:
            across = pick(count, ahead, behind)
            pairs = [(position, (position + 2) % count) for position in (2, 3, 6, 7)]
            pairs += [(b, a) for a, b in pairs]
            blocks.append(lax.ppermute(across, axis, [(ring[a], ring[b]) for a, b in pairs]))
        ahead, behind = step(ahead, 1), step(behind, -1)
        ahead, part = lax.optimization_barrier((ahead, part))
        behind, part = lax.optimization_barrier((behind, part))
        blocks += [ahead, behind]
        fetched.append(part)
    return [b[None] for b in blocks], fetched


def assemble_kernel(packing, tile, per_column, *refs):
    *piece_refs, right_ref, left_ref = refs
    count = sum(ref.shape[0] for ref in piece_refs)
    at = 0
    for ref in piece_refs:
        for p in range(ref.shape[0]):
            right_ref[at * packing.full : (at + 1) * packing.full, :] = ref[p, :, : packing.width]
            for i in range(packing.fold if packing.rest else 0):
                lanes = slice(i * packing.chunk, (i + 1) * packing.chunk)
                low = count * packing.full + at * packing.rest
                right_ref[low : low + packing.rest, lanes] = ref[
                    p, i * packing.rest : (i + 1) * packing.rest, packing.width :
                ]
            at += 1
    start = pl.multiple_of(lax.axis_index("row") % per_column * tile, 128)
    left_ref[...] = right_ref[:, pl.ds(start, tile)]


def assemble(packing, pieces, tile, per_column):
    depth = packing.rows * sum(p.shape[0] for p in pieces)
    dtype = pieces[0].dtype
    return pl.pallas_call(
        functools.partial(assemble_kernel, packing, tile, per_column),
        in_specs=[WHOLE] * len(pieces),
        out_specs=(WHOLE, WHOLE),
        out_shape=(pltpu.VMEM((depth, packing.width), dtype), pltpu.VMEM((depth, tile), dtype)),
        compiler_params=pltpu.CompilerParams(vmem_limit_bytes=8 * MIB),
        name="assemble",
    )(*[in_vmem(p) for p in pieces])


def assemble_plain(packing, pieces, tile, per_column):
    stack = jnp.concatenate(pieces, axis=0)
    count = stack.shape[0]
    top = stack[:, :, : packing.width].reshape(count * packing.full, packing.width)
    rest = stack[:, :, packing.width :].reshape(count, packing.fold, packing.rest, packing.chunk)
    rest = jnp.transpose(rest, (0, 2, 1, 3)).reshape(count * packing.rest, packing.width)
    right = jnp.concatenate([top, rest], axis=0)
    start = lax.axis_index("row") % per_column * tile
    return right, lax.dynamic_slice(right, (0, start), (right.shape[0], tile))


def update_kernel(columns, per_column, schur_hbm, own_ref, peer_ref, right_ref, *refs):
    count = (len(refs) - 5) // 2
    parts, out_ref, held = refs[:count], refs[count], list(refs[count + 1 : 2 * count + 1])
    left, late, sems, late_sem = refs[2 * count + 1 :]
    width = out_ref.shape[1]
    late_rows = out_ref.shape[0] - sum(part.shape[0] for part in parts)
    owner = lax.axis_index("col") == lax.axis_index("row") // per_column
    if late_rows:
        fill = pltpu.make_async_copy(schur_hbm.at[pl.ds(out_ref.shape[0] - late_rows, late_rows), :], late, late_sem)
        fill.start()
        parts, held = [*parts, late], [*held, late]
    steps = width // columns
    lows = [sum(part.shape[0] for part in parts[:i]) for i in range(len(parts))]

    def copy(number, t):
        rows = parts[number].shape[0]
        lanes = pl.ds(pl.multiple_of(t * columns, columns), columns)
        return pltpu.make_async_copy(
            held[number].at[:, lanes], out_ref.at[pl.ds(lows[number], rows), lanes], sems.at[number, t]
        )

    for number, part in enumerate(parts):
        low, rows = lows[number], part.shape[0]

        @pl.when(owner)
        def _():
            left[:rows, :] = own_ref[:, low : low + rows].T

        @pl.when(jnp.logical_not(owner))
        def _():
            left[:rows, :] = peer_ref[:, low : low + rows].T

        if late_rows and number == len(parts) - 1:
            fill.wait()

        def step(t, _):
            lanes = pl.ds(pl.multiple_of(t * columns, columns), columns)
            update = jnp.dot(left[:rows, :], right_ref[:, lanes], preferred_element_type=jnp.float32)
            held[number][:, lanes] = part[:, lanes] - update
            copy(number, t).start()
            return 0

        lax.fori_loop(0, steps, step, 0)
    for number in range(len(parts)):
        for t in range(steps):
            copy(number, t).wait()


def update(schur, parts, own, peer, right, per_column):
    depth, width = right.shape
    tile = schur.shape[0]
    late_rows = tile - sum(part.shape[0] for part in parts)
    columns = next(c for c in (COLS, 256, 128) if width % c == 0)
    most = max([part.shape[0] for part in parts] + [late_rows])
    scratch = 2 * most * max(depth, 128) + 4 * late_rows * width
    result, *_ = pl.pallas_call(
        functools.partial(update_kernel, columns, per_column),
        in_specs=[IN_HBM] + [WHOLE] * (3 + len(parts)),
        out_specs=[ANYWHERE] + [WHOLE] * len(parts),
        out_shape=[jax.ShapeDtypeStruct(schur.shape, schur.dtype)] + [pltpu.VMEM(p.shape, p.dtype) for p in parts],
        input_output_aliases={4 + i: 1 + i for i in range(len(parts))},
        scratch_shapes=[
            pltpu.VMEM((most, depth), right.dtype),
            pltpu.VMEM((late_rows or 8, width), jnp.float32),
            pltpu.SemaphoreType.DMA((len(parts) + 1, width // columns)),
            pltpu.SemaphoreType.DMA,
        ],
        compiler_params=pltpu.CompilerParams(vmem_limit_bytes=scratch + 4 * MIB),
        name="update",
    )(in_hbm(schur), *[in_vmem(a) for a in (own, peer, right, *parts)])
    return result


def per_device(schur_block, w_first, w_second):
    row_count = lax.axis_size("row")
    col_count = lax.axis_size("col")
    tile, width = schur_block.shape
    per_column = row_count // col_count
    packing = Packing(w_first.shape[0] + w_second.shape[0], width)
    sizes, beside_swap = shares_of(tile, row_count // 2)
    packed, room = pack(packing, w_first, w_second, schur_block, sum(sizes[:-1]), sizes[-1] if sizes else 8)
    pieces, parts = gather_rows(packed, "row", schur_block, room, sizes)
    build = assemble if tile % 128 == 0 else assemble_plain
    right, own = build(packing, pieces, tile, per_column)
    if beside_swap:
        parts = [*parts, fetch(schur_block, sum(sizes), beside_swap, own)]
    peer = lax.ppermute(own, "col", [(c, (c + 1) % col_count) for c in range(col_count)])
    return update(schur_block, parts, own, peer, right, per_column)


def solution(mesh):
    assert mesh.shape["col"] == 2
    placed = P(("sup", "row"), "col")
    return jax.shard_map(per_device, mesh=mesh, in_specs=(placed,) * 3, out_specs=placed, check_vma=False)
```

```python
import functools

import jax
import jax.numpy as jnp
from jax import lax
from jax.experimental import pallas as pl
from jax.experimental.pallas import tpu as pltpu
from jax.sharding import PartitionSpec as P

MIB = 1 << 20
WHOLE = pl.BlockSpec(memory_space=pltpu.VMEM)
ANYWHERE = pl.BlockSpec(memory_space=pl.ANY)
IN_HBM = pl.BlockSpec(memory_space=pltpu.HBM)
SHARES = ([11, 11, 18], 4, 4)
COLS = 1024
EARLY = 128


def in_vmem(array):
    return pltpu.with_memory_space_constraint(array, pltpu.VMEM)


def in_hbm(array):
    return pltpu.with_memory_space_constraint(array, pltpu.HBM)


class Packing:
    def __init__(self, rows, width):
        self.rows, self.width = rows, width
        self.full = rows // 8 * 8
        self.rest = rows - self.full
        self.fold = 8 // self.rest if self.rest else 1
        assert self.rest == 0 or (8 % self.rest == 0 and self.full == 8)
        assert width % (128 * self.fold) == 0
        self.chunk = width // self.fold
        self.packed = (self.full, width + (self.chunk if self.rest else 0))


def is_early():
    return jnp.logical_and(lax.axis_index("sup") == 0, lax.axis_index("row") == 0)


def pack_kernel(packing, low, first_ref, second_ref, schur_hbm, out_ref, room_ref, sem):
    rows = min(EARLY, room_ref.shape[0])
    ahead = pltpu.make_async_copy(schur_hbm.at[pl.ds(low, rows), :], room_ref.at[pl.ds(0, rows), :], sem)
    pl.when(is_early())(ahead.start)
    both = jnp.concatenate([first_ref[...], second_ref[...]], axis=0)
    out_ref[:, : packing.width] = both[: packing.full]
    for i in range(packing.fold if packing.rest else 0):
        lanes = slice(i * packing.chunk, (i + 1) * packing.chunk)
        out_ref[i * packing.rest : (i + 1) * packing.rest, packing.width :] = both[packing.full :, lanes]
    pl.when(is_early())(ahead.wait)


def pack(packing, first, second, schur, low, rows):
    return pl.pallas_call(
        functools.partial(pack_kernel, packing, low),
        in_specs=[WHOLE, WHOLE, IN_HBM],
        out_specs=(WHOLE, WHOLE),
        out_shape=(pltpu.VMEM(packing.packed, first.dtype), pltpu.VMEM((rows, schur.shape[1]), schur.dtype)),
        scratch_shapes=[pltpu.SemaphoreType.DMA],
        compiler_params=pltpu.CompilerParams(vmem_limit_bytes=8 * MIB),
        name="pack",
    )(in_hbm(first), in_hbm(second), in_hbm(schur))


def fetch_kernel(low, schur_ref, token_ref, out_ref, sem):
    copy = pltpu.make_async_copy(schur_ref.at[pl.ds(low, out_ref.shape[0]), :], out_ref, sem)
    copy.start()
    copy.wait()


def fetch(schur, low, rows, token):
    width = schur.shape[1]
    return pl.pallas_call(
        functools.partial(fetch_kernel, low),
        in_specs=[IN_HBM, ANYWHERE],
        out_specs=WHOLE,
        out_shape=pltpu.VMEM((rows, width), schur.dtype),
        scratch_shapes=[pltpu.SemaphoreType.DMA],
        cost_estimate=pl.CostEstimate(flops=0, transcendentals=0, bytes_accessed=8 * rows * width),
        compiler_params=pltpu.CompilerParams(vmem_limit_bytes=MIB),
        name="fetch",
    )(in_hbm(schur), token)


def fill_kernel(low, schur_ref, token_ref, room_ref, out_ref, sem):
    rows = out_ref.shape[0]
    skip = min(EARLY, rows)

    def run(done):
        copy = pltpu.make_async_copy(
            schur_ref.at[pl.ds(low + done, rows - done), :], out_ref.at[pl.ds(done, rows - done), :], sem
        )
        copy.start()
        copy.wait()

    if rows > skip:
        pl.when(is_early())(functools.partial(run, skip))
    pl.when(jnp.logical_not(is_early()))(functools.partial(run, 0))


def fill(schur, low, room, token):
    rows, width = room.shape
    return pl.pallas_call(
        functools.partial(fill_kernel, low),
        in_specs=[IN_HBM, ANYWHERE, WHOLE],
        out_specs=WHOLE,
        out_shape=pltpu.VMEM(room.shape, room.dtype),
        input_output_aliases={2: 0},
        scratch_shapes=[pltpu.SemaphoreType.DMA],
        cost_estimate=pl.CostEstimate(flops=0, transcendentals=0, bytes_accessed=8 * rows * width),
        compiler_params=pltpu.CompilerParams(vmem_limit_bytes=MIB),
        name="fill",
    )(in_hbm(schur), token, in_vmem(room))


def shares_of(rows, hops):
    by_hop, by_swap, late = SHARES
    unit = rows // (sum(by_hop) + by_swap + late)
    if hops != 4 or unit % 16 or unit * (sum(by_hop) + by_swap + late) != rows:
        return [], rows
    return [s * unit for s in by_hop], by_swap * unit


def pick_kernel(count, ahead_ref, behind_ref, out_ref):
    index = lax.axis_index("row")
    end = (index >= count // 2) == (index % 2 == 1)

    @pl.when(end)
    def _():
        out_ref[...] = behind_ref[...]

    @pl.when(jnp.logical_not(end))
    def _():
        out_ref[...] = ahead_ref[...]


def pick(count, ahead, behind):
    return pl.pallas_call(
        functools.partial(pick_kernel, count),
        in_specs=[WHOLE] * 2,
        out_specs=WHOLE,
        out_shape=pltpu.VMEM(ahead.shape, ahead.dtype),
        compiler_params=pltpu.CompilerParams(vmem_limit_bytes=MIB),
        name="pick",
    )(in_vmem(ahead), in_vmem(behind))


def gather_rows(block, axis, schur, room, sizes):
    count = lax.axis_size(axis)
    if not sizes:
        return [lax.all_gather(block, axis, axis=0)], []
    assert count == 8
    ring = [2 * i for i in range(count // 2)] + [2 * i + 1 for i in reversed(range(count // 2))]
    place = {index: position for position, index in enumerate(ring)}

    def step(array, by):
        return lax.ppermute(array, axis, [(i, ring[(place[i] + by) % count]) for i in range(count)])

    blocks, ahead, behind, fetched = [block], block, block, []
    for hop in range(3):
        low = sum(sizes[:hop])
        part = fetch(schur, low, sizes[hop], ahead) if hop < 2 else fill(schur, low, room, ahead)
        if hop == 2:
            across = pick(count, ahead, behind)
            pairs = [(position, (position + 2) % count) for position in (2, 3, 6, 7)]
            pairs += [(b, a) for a, b in pairs]
            blocks.append(lax.ppermute(across, axis, [(ring[a], ring[b]) for a, b in pairs]))
        ahead, behind = step(ahead, 1), step(behind, -1)
        ahead, part = lax.optimization_barrier((ahead, part))
        behind, part = lax.optimization_barrier((behind, part))
        blocks += [ahead, behind]
        fetched.append(part)
    return [b[None] for b in blocks], fetched


def assemble_kernel(packing, tile, per_column, *refs):
    *piece_refs, right_ref, left_ref = refs
    count = sum(ref.shape[0] for ref in piece_refs)
    at = 0
    for ref in piece_refs:
        for p in range(ref.shape[0]):
            right_ref[at * packing.full : (at + 1) * packing.full, :] = ref[p, :, : packing.width]
            for i in range(packing.fold if packing.rest else 0):
                lanes = slice(i * packing.chunk, (i + 1) * packing.chunk)
                low = count * packing.full + at * packing.rest
                right_ref[low : low + packing.rest, lanes] = ref[
                    p, i * packing.rest : (i + 1) * packing.rest, packing.width :
                ]
            at += 1
    start = pl.multiple_of(lax.axis_index("row") % per_column * tile, 128)
    left_ref[...] = right_ref[:, pl.ds(start, tile)]


def assemble(packing, pieces, tile, per_column):
    depth = packing.rows * sum(p.shape[0] for p in pieces)
    dtype = pieces[0].dtype
    return pl.pallas_call(
        functools.partial(assemble_kernel, packing, tile, per_column),
        in_specs=[WHOLE] * len(pieces),
        out_specs=(WHOLE, WHOLE),
        out_shape=(pltpu.VMEM((depth, packing.width), dtype), pltpu.VMEM((depth, tile), dtype)),
        compiler_params=pltpu.CompilerParams(vmem_limit_bytes=8 * MIB),
        name="assemble",
    )(*[in_vmem(p) for p in pieces])


def assemble_plain(packing, pieces, tile, per_column):
    stack = jnp.concatenate(pieces, axis=0)
    count = stack.shape[0]
    top = stack[:, :, : packing.width].reshape(count * packing.full, packing.width)
    rest = stack[:, :, packing.width :].reshape(count, packing.fold, packing.rest, packing.chunk)
    rest = jnp.transpose(rest, (0, 2, 1, 3)).reshape(count * packing.rest, packing.width)
    right = jnp.concatenate([top, rest], axis=0)
    start = lax.axis_index("row") % per_column * tile
    return right, lax.dynamic_slice(right, (0, start), (right.shape[0], tile))


def update_kernel(columns, per_column, schur_hbm, own_ref, peer_ref, right_ref, *refs):
    count = (len(refs) - 5) // 2
    parts, out_ref, held = refs[:count], refs[count], list(refs[count + 1 : 2 * count + 1])
    left, late, sems, late_sem = refs[2 * count + 1 :]
    width = out_ref.shape[1]
    late_rows = out_ref.shape[0] - sum(part.shape[0] for part in parts)
    owner = lax.axis_index("col") == lax.axis_index("row") // per_column
    if late_rows:
        fill = pltpu.make_async_copy(schur_hbm.at[pl.ds(out_ref.shape[0] - late_rows, late_rows), :], late, late_sem)
        fill.start()
        parts, held = [*parts, late], [*held, late]
    steps = width // columns
    lows = [sum(part.shape[0] for part in parts[:i]) for i in range(len(parts))]

    def copy(number, t):
        rows = parts[number].shape[0]
        lanes = pl.ds(pl.multiple_of(t * columns, columns), columns)
        return pltpu.make_async_copy(
            held[number].at[:, lanes], out_ref.at[pl.ds(lows[number], rows), lanes], sems.at[number, t]
        )

    for number, part in enumerate(parts):
        low, rows = lows[number], part.shape[0]

        @pl.when(owner)
        def _():
            left[:rows, :] = own_ref[:, low : low + rows].T

        @pl.when(jnp.logical_not(owner))
        def _():
            left[:rows, :] = peer_ref[:, low : low + rows].T

        if late_rows and number == len(parts) - 1:
            fill.wait()

        def step(t, _):
            lanes = pl.ds(pl.multiple_of(t * columns, columns), columns)
            update = jnp.dot(left[:rows, :], right_ref[:, lanes], preferred_element_type=jnp.float32)
            held[number][:, lanes] = part[:, lanes] - update
            copy(number, t).start()
            return 0

        lax.fori_loop(0, steps, step, 0)
    for number in range(len(parts)):
        for t in range(steps):
            copy(number, t).wait()


def update(schur, parts, own, peer, right, per_column):
    depth, width = right.shape
    tile = schur.shape[0]
    late_rows = tile - sum(part.shape[0] for part in parts)
    columns = next(c for c in (COLS, 256, 128) if width % c == 0)
    most = max([part.shape[0] for part in parts] + [late_rows])
    scratch = 2 * most * max(depth, 128) + 4 * late_rows * width
    result, *_ = pl.pallas_call(
        functools.partial(update_kernel, columns, per_column),
        in_specs=[IN_HBM] + [WHOLE] * (3 + len(parts)),
        out_specs=[ANYWHERE] + [WHOLE] * len(parts),
        out_shape=[jax.ShapeDtypeStruct(schur.shape, schur.dtype)] + [pltpu.VMEM(p.shape, p.dtype) for p in parts],
        input_output_aliases={4 + i: 1 + i for i in range(len(parts))},
        scratch_shapes=[
            pltpu.VMEM((most, depth), right.dtype),
            pltpu.VMEM((late_rows or 8, width), jnp.float32),
            pltpu.SemaphoreType.DMA((len(parts) + 1, width // columns)),
            pltpu.SemaphoreType.DMA,
        ],
        compiler_params=pltpu.CompilerParams(vmem_limit_bytes=scratch + 4 * MIB),
        name="update",
    )(in_hbm(schur), *[in_vmem(a) for a in (own, peer, right, *parts)])
    return result


def per_device(schur_block, w_first, w_second):
    row_count = lax.axis_size("row")
    col_count = lax.axis_size("col")
    tile, width = schur_block.shape
    per_column = row_count // col_count
    packing = Packing(w_first.shape[0] + w_second.shape[0], width)
    sizes, beside_swap = shares_of(tile, row_count // 2)
    packed, room = pack(packing, w_first, w_second, schur_block, sum(sizes[:-1]), sizes[-1] if sizes else 8)
    pieces, parts = gather_rows(packed, "row", schur_block, room, sizes)
    build = assemble if tile % 128 == 0 else assemble_plain
    right, own = build(packing, pieces, tile, per_column)
    if beside_swap:
        parts = [*parts, fetch(schur_block, sum(sizes), beside_swap, own)]
    peer = lax.ppermute(own, "col", [(c, (c + 1) % col_count) for c in range(col_count)])
    return update(schur_block, parts, own, peer, right, per_column)


def solution(mesh):
    assert mesh.shape["col"] == 2
    placed = P(("sup", "row"), "col")
    return jax.shard_map(per_device, mesh=mesh, in_specs=(placed,) * 3, out_specs=placed, check_vma=False)
```

```python
import functools

import jax
import jax.numpy as jnp
from jax import lax
from jax.experimental import pallas as pl
from jax.experimental.pallas import tpu as pltpu
from jax.sharding import PartitionSpec as P

MIB = 1 << 20
WHOLE = pl.BlockSpec(memory_space=pltpu.VMEM)
ANYWHERE = pl.BlockSpec(memory_space=pl.ANY)
IN_HBM = pl.BlockSpec(memory_space=pltpu.HBM)
SHARES = ([11, 11, 18], 4, 4)
COLS = 1024
EARLY = 128
WAITING = 48


def in_vmem(array):
    return pltpu.with_memory_space_constraint(array, pltpu.VMEM)


def in_hbm(array):
    return pltpu.with_memory_space_constraint(array, pltpu.HBM)


class Packing:
    def __init__(self, rows, width):
        self.rows, self.width = rows, width
        self.full = rows // 8 * 8
        self.rest = rows - self.full
        self.fold = 8 // self.rest if self.rest else 1
        assert self.rest == 0 or (8 % self.rest == 0 and self.full == 8)
        assert width % (128 * self.fold) == 0
        self.chunk = width // self.fold
        self.packed = (self.full, width + (self.chunk if self.rest else 0))


def is_early():
    return jnp.logical_and(lax.axis_index("sup") == 0, lax.axis_index("row") == 0)


def pack_kernel(packing, low, first_ref, second_ref, schur_hbm, out_ref, room_ref, sem):
    rows = min(EARLY, room_ref.shape[0])
    ahead = pltpu.make_async_copy(schur_hbm.at[pl.ds(low, rows), :], room_ref.at[pl.ds(0, rows), :], sem)
    pl.when(is_early())(ahead.start)
    both = jnp.concatenate([first_ref[...], second_ref[...]], axis=0)
    out_ref[:, : packing.width] = both[: packing.full]
    for i in range(packing.fold if packing.rest else 0):
        lanes = slice(i * packing.chunk, (i + 1) * packing.chunk)
        out_ref[i * packing.rest : (i + 1) * packing.rest, packing.width :] = both[packing.full :, lanes]
    pl.when(is_early())(ahead.wait)


def pack(packing, first, second, schur, low, rows):
    return pl.pallas_call(
        functools.partial(pack_kernel, packing, low),
        in_specs=[WHOLE, WHOLE, IN_HBM],
        out_specs=(WHOLE, WHOLE),
        out_shape=(pltpu.VMEM(packing.packed, first.dtype), pltpu.VMEM((rows, schur.shape[1]), schur.dtype)),
        scratch_shapes=[pltpu.SemaphoreType.DMA],
        compiler_params=pltpu.CompilerParams(vmem_limit_bytes=8 * MIB),
        name="pack",
    )(in_hbm(first), in_hbm(second), in_hbm(schur))


def fetch_kernel(low, schur_ref, token_ref, out_ref, sem):
    copy = pltpu.make_async_copy(schur_ref.at[pl.ds(low, out_ref.shape[0]), :], out_ref, sem)
    copy.start()
    copy.wait()


def fetch(schur, low, rows, token):
    width = schur.shape[1]
    return pl.pallas_call(
        functools.partial(fetch_kernel, low),
        in_specs=[IN_HBM, ANYWHERE],
        out_specs=WHOLE,
        out_shape=pltpu.VMEM((rows, width), schur.dtype),
        scratch_shapes=[pltpu.SemaphoreType.DMA],
        cost_estimate=pl.CostEstimate(flops=0, transcendentals=0, bytes_accessed=8 * rows * width),
        compiler_params=pltpu.CompilerParams(vmem_limit_bytes=MIB),
        name="fetch",
    )(in_hbm(schur), token)


def fill_kernel(low, schur_ref, token_ref, room_ref, out_ref, sem):
    rows = out_ref.shape[0]

    def run(done):
        copy = pltpu.make_async_copy(
            schur_ref.at[pl.ds(low + done, rows - done), :], out_ref.at[pl.ds(done, rows - done), :], sem
        )
        copy.start()
        copy.wait()

    early, waiting = is_early(), is_waiting()
    pl.when(early)(functools.partial(run, EARLY))
    pl.when(waiting)(functools.partial(run, WAITING))
    pl.when(jnp.logical_not(jnp.logical_or(early, waiting)))(functools.partial(run, 0))


def fill(schur, low, room, token):
    rows, width = room.shape
    return pl.pallas_call(
        functools.partial(fill_kernel, low),
        in_specs=[IN_HBM, ANYWHERE, WHOLE],
        out_specs=WHOLE,
        out_shape=pltpu.VMEM(room.shape, room.dtype),
        input_output_aliases={2: 0},
        scratch_shapes=[pltpu.SemaphoreType.DMA],
        cost_estimate=pl.CostEstimate(flops=0, transcendentals=0, bytes_accessed=8 * rows * width),
        compiler_params=pltpu.CompilerParams(vmem_limit_bytes=MIB),
        name="fill",
    )(in_hbm(schur), token, in_vmem(room))


def shares_of(rows, hops):
    by_hop, by_swap, late = SHARES
    unit = rows // (sum(by_hop) + by_swap + late)
    if hops != 4 or unit % 16 or unit * (sum(by_hop) + by_swap + late) != rows:
        return [], rows
    assert by_hop[-1] * unit > max(EARLY, WAITING)
    return [s * unit for s in by_hop], by_swap * unit


def is_waiting():
    return jnp.logical_and(lax.axis_index("row") % 4 == 0, jnp.logical_not(is_early()))


def pick_kernel(low, ahead_ref, behind_ref, schur_ref, room_ref, out_ref, filled_ref, sem):
    index = lax.axis_index("row")
    end = (index >= lax.axis_size("row") // 2) == (index % 2 == 1)

    @pl.when(end)
    def _():
        out_ref[...] = behind_ref[...]

    @pl.when(jnp.logical_not(end))
    def _():
        out_ref[...] = ahead_ref[...]

    def run(done):
        rows = pl.ds(done, WAITING)
        copy = pltpu.make_async_copy(schur_ref.at[pl.ds(low + done, WAITING), :], filled_ref.at[rows, :], sem)
        copy.start()
        copy.wait()

    pl.when(is_waiting())(functools.partial(run, 0))


def pick(low, ahead, behind, schur, room):
    return pl.pallas_call(
        functools.partial(pick_kernel, low),
        in_specs=[WHOLE, WHOLE, IN_HBM, WHOLE],
        out_specs=(WHOLE, WHOLE),
        out_shape=(pltpu.VMEM(ahead.shape, ahead.dtype), pltpu.VMEM(room.shape, room.dtype)),
        input_output_aliases={3: 1},
        scratch_shapes=[pltpu.SemaphoreType.DMA],
        compiler_params=pltpu.CompilerParams(vmem_limit_bytes=MIB),
        name="pick",
    )(in_vmem(ahead), in_vmem(behind), in_hbm(schur), in_vmem(room))


def gather_rows(block, axis, schur, room, sizes):
    count = lax.axis_size(axis)
    if not sizes:
        return [lax.all_gather(block, axis, axis=0)], []
    assert count == 8
    ring = [2 * i for i in range(count // 2)] + [2 * i + 1 for i in reversed(range(count // 2))]
    place = {index: position for position, index in enumerate(ring)}

    def step(array, by):
        return lax.ppermute(array, axis, [(i, ring[(place[i] + by) % count]) for i in range(count)])

    blocks, ahead, behind, fetched = [block], block, block, []
    for hop in range(3):
        low = sum(sizes[:hop])
        if hop < 2:
            part = fetch(schur, low, sizes[hop], ahead)
        else:
            across, room = pick(low, ahead, behind, schur, room)
            part = fill(schur, low, room, across)
            pairs = [(position, (position + 2) % count) for position in (2, 3, 6, 7)]
            pairs += [(b, a) for a, b in pairs]
            blocks.append(lax.ppermute(across, axis, [(ring[a], ring[b]) for a, b in pairs]))
        ahead, behind = step(ahead, 1), step(behind, -1)
        ahead, part = lax.optimization_barrier((ahead, part))
        behind, part = lax.optimization_barrier((behind, part))
        blocks += [ahead, behind]
        fetched.append(part)
    return [b[None] for b in blocks], fetched


def assemble_kernel(packing, tile, per_column, *refs):
    *piece_refs, right_ref, left_ref = refs
    count = sum(ref.shape[0] for ref in piece_refs)
    at = 0
    for ref in piece_refs:
        for p in range(ref.shape[0]):
            right_ref[at * packing.full : (at + 1) * packing.full, :] = ref[p, :, : packing.width]
            for i in range(packing.fold if packing.rest else 0):
                lanes = slice(i * packing.chunk, (i + 1) * packing.chunk)
                low = count * packing.full + at * packing.rest
                right_ref[low : low + packing.rest, lanes] = ref[
                    p, i * packing.rest : (i + 1) * packing.rest, packing.width :
                ]
            at += 1
    start = pl.multiple_of(lax.axis_index("row") % per_column * tile, 128)
    left_ref[...] = right_ref[:, pl.ds(start, tile)]


def assemble(packing, pieces, tile, per_column):
    depth = packing.rows * sum(p.shape[0] for p in pieces)
    dtype = pieces[0].dtype
    return pl.pallas_call(
        functools.partial(assemble_kernel, packing, tile, per_column),
        in_specs=[WHOLE] * len(pieces),
        out_specs=(WHOLE, WHOLE),
        out_shape=(pltpu.VMEM((depth, packing.width), dtype), pltpu.VMEM((depth, tile), dtype)),
        compiler_params=pltpu.CompilerParams(vmem_limit_bytes=8 * MIB),
        name="assemble",
    )(*[in_vmem(p) for p in pieces])


def assemble_plain(packing, pieces, tile, per_column):
    stack = jnp.concatenate(pieces, axis=0)
    count = stack.shape[0]
    top = stack[:, :, : packing.width].reshape(count * packing.full, packing.width)
    rest = stack[:, :, packing.width :].reshape(count, packing.fold, packing.rest, packing.chunk)
    rest = jnp.transpose(rest, (0, 2, 1, 3)).reshape(count * packing.rest, packing.width)
    right = jnp.concatenate([top, rest], axis=0)
    start = lax.axis_index("row") % per_column * tile
    return right, lax.dynamic_slice(right, (0, start), (right.shape[0], tile))


def update_kernel(columns, per_column, schur_hbm, own_ref, peer_ref, right_ref, *refs):
    count = (len(refs) - 5) // 2
    parts, out_ref, held = refs[:count], refs[count], list(refs[count + 1 : 2 * count + 1])
    left, late, sems, late_sem = refs[2 * count + 1 :]
    width = out_ref.shape[1]
    late_rows = out_ref.shape[0] - sum(part.shape[0] for part in parts)
    owner = lax.axis_index("col") == lax.axis_index("row") // per_column
    if late_rows:
        fill = pltpu.make_async_copy(schur_hbm.at[pl.ds(out_ref.shape[0] - late_rows, late_rows), :], late, late_sem)
        fill.start()
        parts, held = [*parts, late], [*held, late]
    steps = width // columns
    lows = [sum(part.shape[0] for part in parts[:i]) for i in range(len(parts))]

    def copy(number, t):
        rows = parts[number].shape[0]
        lanes = pl.ds(pl.multiple_of(t * columns, columns), columns)
        return pltpu.make_async_copy(
            held[number].at[:, lanes], out_ref.at[pl.ds(lows[number], rows), lanes], sems.at[number, t]
        )

    for number, part in enumerate(parts):
        low, rows = lows[number], part.shape[0]

        @pl.when(owner)
        def _():
            left[:rows, :] = own_ref[:, low : low + rows].T

        @pl.when(jnp.logical_not(owner))
        def _():
            left[:rows, :] = peer_ref[:, low : low + rows].T

        if late_rows and number == len(parts) - 1:
            fill.wait()

        def step(t, _):
            lanes = pl.ds(pl.multiple_of(t * columns, columns), columns)
            update = jnp.dot(left[:rows, :], right_ref[:, lanes], preferred_element_type=jnp.float32)
            held[number][:, lanes] = part[:, lanes] - update
            copy(number, t).start()
            return 0

        lax.fori_loop(0, steps, step, 0)
    for number in range(len(parts)):
        for t in range(steps):
            copy(number, t).wait()


def update(schur, parts, own, peer, right, per_column):
    depth, width = right.shape
    tile = schur.shape[0]
    late_rows = tile - sum(part.shape[0] for part in parts)
    columns = next(c for c in (COLS, 256, 128) if width % c == 0)
    most = max([part.shape[0] for part in parts] + [late_rows])
    scratch = 2 * most * max(depth, 128) + 4 * late_rows * width
    result, *_ = pl.pallas_call(
        functools.partial(update_kernel, columns, per_column),
        in_specs=[IN_HBM] + [WHOLE] * (3 + len(parts)),
        out_specs=[ANYWHERE] + [WHOLE] * len(parts),
        out_shape=[jax.ShapeDtypeStruct(schur.shape, schur.dtype)] + [pltpu.VMEM(p.shape, p.dtype) for p in parts],
        input_output_aliases={4 + i: 1 + i for i in range(len(parts))},
        scratch_shapes=[
            pltpu.VMEM((most, depth), right.dtype),
            pltpu.VMEM((late_rows or 8, width), jnp.float32),
            pltpu.SemaphoreType.DMA((len(parts) + 1, width // columns)),
            pltpu.SemaphoreType.DMA,
        ],
        compiler_params=pltpu.CompilerParams(vmem_limit_bytes=scratch + 4 * MIB),
        name="update",
    )(in_hbm(schur), *[in_vmem(a) for a in (own, peer, right, *parts)])
    return result


def per_device(schur_block, w_first, w_second):
    row_count = lax.axis_size("row")
    col_count = lax.axis_size("col")
    tile, width = schur_block.shape
    per_column = row_count // col_count
    packing = Packing(w_first.shape[0] + w_second.shape[0], width)
    sizes, beside_swap = shares_of(tile, row_count // 2)
    packed, room = pack(packing, w_first, w_second, schur_block, sum(sizes[:-1]), sizes[-1] if sizes else 8)
    pieces, parts = gather_rows(packed, "row", schur_block, room, sizes)
    build = assemble if tile % 128 == 0 else assemble_plain
    right, own = build(packing, pieces, tile, per_column)
    if beside_swap:
        parts = [*parts, fetch(schur_block, sum(sizes), beside_swap, own)]
    peer = lax.ppermute(own, "col", [(c, (c + 1) % col_count) for c in range(col_count)])
    return update(schur_block, parts, own, peer, right, per_column)


def solution(mesh):
    assert mesh.shape["col"] == 2
    placed = P(("sup", "row"), "col")
    return jax.shard_map(per_device, mesh=mesh, in_specs=(placed,) * 3, out_specs=placed, check_vma=False)
```

```python
import functools

import jax
import jax.numpy as jnp
from jax import lax
from jax.experimental import pallas as pl
from jax.experimental.pallas import tpu as pltpu
from jax.sharding import PartitionSpec as P

MIB = 1 << 20
WHOLE = pl.BlockSpec(memory_space=pltpu.VMEM)
ANYWHERE = pl.BlockSpec(memory_space=pl.ANY)
IN_HBM = pl.BlockSpec(memory_space=pltpu.HBM)
SHARES = ([11, 11, 19], 3, 4)
COLS = 1024
EARLY = 128
WAITING = 48


def in_vmem(array):
    return pltpu.with_memory_space_constraint(array, pltpu.VMEM)


def in_hbm(array):
    return pltpu.with_memory_space_constraint(array, pltpu.HBM)


class Packing:
    def __init__(self, rows, width):
        self.rows, self.width = rows, width
        self.full = rows // 8 * 8
        self.rest = rows - self.full
        self.fold = 8 // self.rest if self.rest else 1
        assert self.rest == 0 or (8 % self.rest == 0 and self.full == 8)
        assert width % (128 * self.fold) == 0
        self.chunk = width // self.fold
        self.packed = (self.full, width + (self.chunk if self.rest else 0))


def is_early():
    return jnp.logical_and(lax.axis_index("sup") == 0, lax.axis_index("row") == 0)


def pack_kernel(packing, low, first_ref, second_ref, schur_hbm, out_ref, room_ref, sem):
    rows = min(EARLY, room_ref.shape[0])
    ahead = pltpu.make_async_copy(schur_hbm.at[pl.ds(low, rows), :], room_ref.at[pl.ds(0, rows), :], sem)
    pl.when(is_early())(ahead.start)
    both = jnp.concatenate([first_ref[...], second_ref[...]], axis=0)
    out_ref[:, : packing.width] = both[: packing.full]
    for i in range(packing.fold if packing.rest else 0):
        lanes = slice(i * packing.chunk, (i + 1) * packing.chunk)
        out_ref[i * packing.rest : (i + 1) * packing.rest, packing.width :] = both[packing.full :, lanes]
    pl.when(is_early())(ahead.wait)


def pack(packing, first, second, schur, low, rows):
    return pl.pallas_call(
        functools.partial(pack_kernel, packing, low),
        in_specs=[WHOLE, WHOLE, IN_HBM],
        out_specs=(WHOLE, WHOLE),
        out_shape=(pltpu.VMEM(packing.packed, first.dtype), pltpu.VMEM((rows, schur.shape[1]), schur.dtype)),
        scratch_shapes=[pltpu.SemaphoreType.DMA],
        compiler_params=pltpu.CompilerParams(vmem_limit_bytes=8 * MIB),
        name="pack",
    )(in_hbm(first), in_hbm(second), in_hbm(schur))


def fetch_kernel(low, schur_ref, token_ref, out_ref, sem):
    copy = pltpu.make_async_copy(schur_ref.at[pl.ds(low, out_ref.shape[0]), :], out_ref, sem)
    copy.start()
    copy.wait()


def fetch(schur, low, rows, token):
    width = schur.shape[1]
    return pl.pallas_call(
        functools.partial(fetch_kernel, low),
        in_specs=[IN_HBM, ANYWHERE],
        out_specs=WHOLE,
        out_shape=pltpu.VMEM((rows, width), schur.dtype),
        scratch_shapes=[pltpu.SemaphoreType.DMA],
        cost_estimate=pl.CostEstimate(flops=0, transcendentals=0, bytes_accessed=8 * rows * width),
        compiler_params=pltpu.CompilerParams(vmem_limit_bytes=MIB),
        name="fetch",
    )(in_hbm(schur), token)


def fill_kernel(low, schur_ref, token_ref, room_ref, out_ref, sem):
    rows = out_ref.shape[0]

    def run(done):
        copy = pltpu.make_async_copy(
            schur_ref.at[pl.ds(low + done, rows - done), :], out_ref.at[pl.ds(done, rows - done), :], sem
        )
        copy.start()
        copy.wait()

    early, waiting = is_early(), is_waiting()
    pl.when(early)(functools.partial(run, EARLY))
    pl.when(waiting)(functools.partial(run, WAITING))
    pl.when(jnp.logical_not(jnp.logical_or(early, waiting)))(functools.partial(run, 0))


def fill(schur, low, room, token):
    rows, width = room.shape
    return pl.pallas_call(
        functools.partial(fill_kernel, low),
        in_specs=[IN_HBM, ANYWHERE, WHOLE],
        out_specs=WHOLE,
        out_shape=pltpu.VMEM(room.shape, room.dtype),
        input_output_aliases={2: 0},
        scratch_shapes=[pltpu.SemaphoreType.DMA],
        cost_estimate=pl.CostEstimate(flops=0, transcendentals=0, bytes_accessed=8 * rows * width),
        compiler_params=pltpu.CompilerParams(vmem_limit_bytes=MIB),
        name="fill",
    )(in_hbm(schur), token, in_vmem(room))


def shares_of(rows, hops):
    by_hop, by_swap, late = SHARES
    unit = rows // (sum(by_hop) + by_swap + late)
    if hops != 4 or unit % 16 or unit * (sum(by_hop) + by_swap + late) != rows:
        return [], rows
    assert by_hop[-1] * unit > max(EARLY, WAITING)
    return [s * unit for s in by_hop], by_swap * unit


def is_waiting():
    return jnp.logical_and(lax.axis_index("row") % 4 == 0, jnp.logical_not(is_early()))


def pick_kernel(low, ahead_ref, behind_ref, schur_ref, room_ref, out_ref, filled_ref, sem):
    index = lax.axis_index("row")
    end = (index >= lax.axis_size("row") // 2) == (index % 2 == 1)

    @pl.when(end)
    def _():
        out_ref[...] = behind_ref[...]

    @pl.when(jnp.logical_not(end))
    def _():
        out_ref[...] = ahead_ref[...]

    def run(done):
        rows = pl.ds(done, WAITING)
        copy = pltpu.make_async_copy(schur_ref.at[pl.ds(low + done, WAITING), :], filled_ref.at[rows, :], sem)
        copy.start()
        copy.wait()

    pl.when(is_waiting())(functools.partial(run, 0))


def pick(low, ahead, behind, schur, room):
    return pl.pallas_call(
        functools.partial(pick_kernel, low),
        in_specs=[WHOLE, WHOLE, IN_HBM, WHOLE],
        out_specs=(WHOLE, WHOLE),
        out_shape=(pltpu.VMEM(ahead.shape, ahead.dtype), pltpu.VMEM(room.shape, room.dtype)),
        input_output_aliases={3: 1},
        scratch_shapes=[pltpu.SemaphoreType.DMA],
        compiler_params=pltpu.CompilerParams(vmem_limit_bytes=MIB),
        name="pick",
    )(in_vmem(ahead), in_vmem(behind), in_hbm(schur), in_vmem(room))


def gather_rows(block, axis, schur, room, sizes):
    count = lax.axis_size(axis)
    if not sizes:
        return [lax.all_gather(block, axis, axis=0)], []
    assert count == 8
    ring = [2 * i for i in range(count // 2)] + [2 * i + 1 for i in reversed(range(count // 2))]
    place = {index: position for position, index in enumerate(ring)}

    def step(array, by):
        return lax.ppermute(array, axis, [(i, ring[(place[i] + by) % count]) for i in range(count)])

    blocks, ahead, behind, fetched = [block], block, block, []
    for hop in range(3):
        low = sum(sizes[:hop])
        if hop < 2:
            part = fetch(schur, low, sizes[hop], ahead)
        else:
            across, room = pick(low, ahead, behind, schur, room)
            part = fill(schur, low, room, across)
            pairs = [(position, (position + 2) % count) for position in (2, 3, 6, 7)]
            pairs += [(b, a) for a, b in pairs]
            blocks.append(lax.ppermute(across, axis, [(ring[a], ring[b]) for a, b in pairs]))
        ahead, behind = step(ahead, 1), step(behind, -1)
        ahead, part = lax.optimization_barrier((ahead, part))
        behind, part = lax.optimization_barrier((behind, part))
        blocks += [ahead, behind]
        fetched.append(part)
    return [b[None] for b in blocks], fetched


def assemble_kernel(packing, tile, per_column, *refs):
    *piece_refs, right_ref, left_ref = refs
    count = sum(ref.shape[0] for ref in piece_refs)
    at = 0
    for ref in piece_refs:
        for p in range(ref.shape[0]):
            right_ref[at * packing.full : (at + 1) * packing.full, :] = ref[p, :, : packing.width]
            for i in range(packing.fold if packing.rest else 0):
                lanes = slice(i * packing.chunk, (i + 1) * packing.chunk)
                low = count * packing.full + at * packing.rest
                right_ref[low : low + packing.rest, lanes] = ref[
                    p, i * packing.rest : (i + 1) * packing.rest, packing.width :
                ]
            at += 1
    start = pl.multiple_of(lax.axis_index("row") % per_column * tile, 128)
    left_ref[...] = right_ref[:, pl.ds(start, tile)]


def assemble(packing, pieces, tile, per_column):
    depth = packing.rows * sum(p.shape[0] for p in pieces)
    dtype = pieces[0].dtype
    return pl.pallas_call(
        functools.partial(assemble_kernel, packing, tile, per_column),
        in_specs=[WHOLE] * len(pieces),
        out_specs=(WHOLE, WHOLE),
        out_shape=(pltpu.VMEM((depth, packing.width), dtype), pltpu.VMEM((depth, tile), dtype)),
        compiler_params=pltpu.CompilerParams(vmem_limit_bytes=8 * MIB),
        name="assemble",
    )(*[in_vmem(p) for p in pieces])


def assemble_plain(packing, pieces, tile, per_column):
    stack = jnp.concatenate(pieces, axis=0)
    count = stack.shape[0]
    top = stack[:, :, : packing.width].reshape(count * packing.full, packing.width)
    rest = stack[:, :, packing.width :].reshape(count, packing.fold, packing.rest, packing.chunk)
    rest = jnp.transpose(rest, (0, 2, 1, 3)).reshape(count * packing.rest, packing.width)
    right = jnp.concatenate([top, rest], axis=0)
    start = lax.axis_index("row") % per_column * tile
    return right, lax.dynamic_slice(right, (0, start), (right.shape[0], tile))


def update_kernel(columns, per_column, schur_hbm, own_ref, peer_ref, right_ref, *refs):
    count = (len(refs) - 5) // 2
    parts, out_ref, held = refs[:count], refs[count], list(refs[count + 1 : 2 * count + 1])
    left, late, sems, late_sem = refs[2 * count + 1 :]
    width = out_ref.shape[1]
    late_rows = out_ref.shape[0] - sum(part.shape[0] for part in parts)
    owner = lax.axis_index("col") == lax.axis_index("row") // per_column
    if late_rows:
        fill = pltpu.make_async_copy(schur_hbm.at[pl.ds(out_ref.shape[0] - late_rows, late_rows), :], late, late_sem)
        fill.start()
        parts, held = [*parts, late], [*held, late]
    steps = width // columns
    lows = [sum(part.shape[0] for part in parts[:i]) for i in range(len(parts))]

    def copy(number, t):
        rows = parts[number].shape[0]
        lanes = pl.ds(pl.multiple_of(t * columns, columns), columns)
        return pltpu.make_async_copy(
            held[number].at[:, lanes], out_ref.at[pl.ds(lows[number], rows), lanes], sems.at[number, t]
        )

    for number, part in enumerate(parts):
        low, rows = lows[number], part.shape[0]

        @pl.when(owner)
        def _():
            left[:rows, :] = own_ref[:, low : low + rows].T

        @pl.when(jnp.logical_not(owner))
        def _():
            left[:rows, :] = peer_ref[:, low : low + rows].T

        if late_rows and number == len(parts) - 1:
            fill.wait()

        def step(t, _):
            lanes = pl.ds(pl.multiple_of(t * columns, columns), columns)
            update = jnp.dot(left[:rows, :], right_ref[:, lanes], preferred_element_type=jnp.float32)
            held[number][:, lanes] = part[:, lanes] - update
            copy(number, t).start()
            return 0

        lax.fori_loop(0, steps, step, 0)
    for number in range(len(parts)):
        for t in range(steps):
            copy(number, t).wait()


def update(schur, parts, own, peer, right, per_column):
    depth, width = right.shape
    tile = schur.shape[0]
    late_rows = tile - sum(part.shape[0] for part in parts)
    columns = next(c for c in (COLS, 256, 128) if width % c == 0)
    most = max([part.shape[0] for part in parts] + [late_rows])
    scratch = 2 * most * max(depth, 128) + 4 * late_rows * width
    result, *_ = pl.pallas_call(
        functools.partial(update_kernel, columns, per_column),
        in_specs=[IN_HBM] + [WHOLE] * (3 + len(parts)),
        out_specs=[ANYWHERE] + [WHOLE] * len(parts),
        out_shape=[jax.ShapeDtypeStruct(schur.shape, schur.dtype)] + [pltpu.VMEM(p.shape, p.dtype) for p in parts],
        input_output_aliases={4 + i: 1 + i for i in range(len(parts))},
        scratch_shapes=[
            pltpu.VMEM((most, depth), right.dtype),
            pltpu.VMEM((late_rows or 8, width), jnp.float32),
            pltpu.SemaphoreType.DMA((len(parts) + 1, width // columns)),
            pltpu.SemaphoreType.DMA,
        ],
        compiler_params=pltpu.CompilerParams(vmem_limit_bytes=scratch + 4 * MIB),
        name="update",
    )(in_hbm(schur), *[in_vmem(a) for a in (own, peer, right, *parts)])
    return result


def per_device(schur_block, w_first, w_second):
    row_count = lax.axis_size("row")
    col_count = lax.axis_size("col")
    tile, width = schur_block.shape
    per_column = row_count // col_count
    packing = Packing(w_first.shape[0] + w_second.shape[0], width)
    sizes, beside_swap = shares_of(tile, row_count // 2)
    packed, room = pack(packing, w_first, w_second, schur_block, sum(sizes[:-1]), sizes[-1] if sizes else 8)
    pieces, parts = gather_rows(packed, "row", schur_block, room, sizes)
    build = assemble if tile % 128 == 0 else assemble_plain
    right, own = build(packing, pieces, tile, per_column)
    if beside_swap:
        parts = [*parts, fetch(schur_block, sum(sizes), beside_swap, own)]
    peer = lax.ppermute(own, "col", [(c, (c + 1) % col_count) for c in range(col_count)])
    return update(schur_block, parts, own, peer, right, per_column)


def solution(mesh):
    assert mesh.shape["col"] == 2
    placed = P(("sup", "row"), "col")
    return jax.shard_map(per_device, mesh=mesh, in_specs=(placed,) * 3, out_specs=placed, check_vma=False)
```
